32 devices in a mesh: mp: 8 (over z, x), seq: 4 (over y, core).
Axes of the slice: x: 2, y: 2, z: 4, core: 2. Of those that a mesh axis runs over, the one named last changes fastest.
Arguments:
- hidden_in: bfloat16 [256, 8192], P(None, 'mp'), may hold values from -4 to 4
- attn_gain: bfloat16 [8192], P('mp'), may hold values from 0.099609375 to 1.8984375
- mlp_gain: bfloat16 [8192], replicated, may hold values from 0.099609375 to 1.8984375
- w_query: bfloat16 [8192, 8192], P('mp', 'seq'), may hold values from -1 to 1
- w_key: bfloat16 [8192, 1024], P('mp', 'seq'), may hold values from -1 to 1
- w_value: bfloat16 [8192, 1024], P('mp', 'seq'), may hold values from -0.0625 to 0.0625
- w_out: bfloat16 [8192, 8192], P('seq', 'mp'), may hold values from -0.0625 to 0.0625
- w_gate: bfloat16 [8192, 28672], P(None, ('mp', 'seq')), may hold values from -0.0625 to 0.0625
- w_up: bfloat16 [8192, 28672], P(None, ('mp', 'seq')), may hold values from -0.0625 to 0.0625
- w_down: bfloat16 [28672, 8192], P(('mp', 'seq')), may hold values from -0.03125 to 0.03125
- prompt_cache: bfloat16 [8, 8, 32768, 256], P(None, 'seq', 'mp'), may hold values from -136 to 136
- tail_cache: bfloat16 [128, 8, 512, 256], P('mp', 'seq'), may hold values from -136 to 136
- prompt_len: int32 [8], replicated, may hold values from 4096 to 32768, as said below
- tail_len: int32 [128], replicated, may hold values from 1 to 512, as said below
- prompt_of: int32 [128], replicated, may hold values from 0 to 7, as said below
Outputs:
- layer_out: bfloat16 [256, 8192], P(('mp', 'seq'))
- input_rms: float32 [256], replicated
- max_logit: float32 [128, 64], P(None, 'seq')
- new_entries: bfloat16 [128, 8, 2, 256], P('mp', 'seq')
The draws below stay inside these ranges and needn't reach their ends.
Inputs may be any that keep to these rules, and one draw needn't show every extreme that they name: `prompt_len`: at least one prompt has 32768 positions. `tail_len`: at least one request has 512 tail positions. `prompt_of`: each prompt feeds exactly 16 requests.
All inputs are finite; a program needn't handle non-finite values.
Results may differ from the reference program's by a relative error of at most 0.028.
The reference program's roundings to bfloat16 on the way count: a program that leaves them out, or rounds other values in their place, can miss the bound.
Values may be sent and summed in bfloat16 or wider, within the bound.
A program may use at most 320 MiB of HBM per device.

```python
import jax
import jax.numpy as jnp
from jax import lax

D = 8192
H = 64
KVH = 8
HD = 128
FF = 28672
PLEN = 32768
TLEN = 512
PROMPTS = 8
CONT = 16
QPK = 8
REQ = 128
ROWS = 256


def draw_hidden_in(key, part):
    noise_key, column_key, row_key = jax.random.split(key, 3)
    rising = jnp.exp(jnp.arange(D, dtype=jnp.float32) / D * jnp.log(3.0))
    column_scale = rising[None, :] * jnp.exp(jax.random.uniform(column_key, (1, D), minval=0.0, maxval=jnp.log(4.0)))
    row_scale = jnp.exp(jax.random.uniform(row_key, (ROWS, 1), minval=jnp.log(0.5), maxval=jnp.log(5.0)))
    base_values = jax.random.truncated_normal(noise_key, -6.0, 6.0, (ROWS, D))
    return (0.01 * base_values * column_scale * row_scale).astype(jnp.bfloat16)


def query_matrix(key):
    return jax.random.truncated_normal(jax.random.fold_in(key, 11), -6.0, 6.0, (D, H * HD)) * D ** (-0.5)


def draw_w_query(key, part):
    return query_matrix(key).astype(jnp.bfloat16)


def draw_w_key(key, part):
    chosen = jax.random.randint(jax.random.fold_in(key, 13), (KVH,), 0, H // KVH)
    heads = jnp.arange(KVH, dtype=jnp.int32) * (H // KVH) + chosen
    columns = (heads[:, None] * HD + jnp.arange(HD, dtype=jnp.int32)[None, :]).reshape(KVH * HD)
    base_values = query_matrix(key)[:, columns]
    noise = jax.random.truncated_normal(jax.random.fold_in(key, 12), -6.0, 6.0, (D, KVH * HD)) * D ** (-0.5)
    return (0.8 * base_values + 0.6 * noise).astype(jnp.bfloat16)


def draw_prompt_cache(key, part):
    shape = (PROMPTS, KVH, PLEN, 2 * HD)
    value_key = jax.random.fold_in(key, 0)
    base_values = jax.random.truncated_normal(value_key, -6.0, 6.0, shape)
    return base_values.astype(jnp.bfloat16)


def draw_tail_cache(key, part):
    shape = (REQ, KVH, TLEN, 2 * HD)
    value_key = jax.random.fold_in(jax.random.fold_in(key, 29), 0)
    base_values = jax.random.truncated_normal(value_key, -6.0, 6.0, shape)
    return base_values.astype(jnp.bfloat16)


def draw_prompt_len(key, part):
    length_key, pick_key = jax.random.split(key)
    lengths = jax.random.randint(length_key, (PROMPTS,), PLEN // 8, PLEN + 1)
    longest = jax.random.randint(pick_key, (), 0, PROMPTS)
    return jnp.where(jnp.arange(PROMPTS, dtype=jnp.int32) == longest, PLEN, lengths).astype(jnp.int32)


def draw_tail_len(key, part):
    length_key, pick_key = jax.random.split(key)
    lengths = jax.random.randint(length_key, (PROMPTS * CONT,), 1, TLEN + 1)
    longest = jax.random.randint(pick_key, (), 0, PROMPTS * CONT)
    return jnp.where(jnp.arange(PROMPTS * CONT, dtype=jnp.int32) == longest, TLEN, lengths).astype(jnp.int32)


def draw_prompt_of(key, part):
    shuffled = jax.random.permutation(key, PROMPTS * CONT)
    return (shuffled // CONT).astype(jnp.int32)


def levels(key, dims, cuts, smallest, high):
    def one(dim, parts):
        steps = jax.random.uniform(jax.random.fold_in(jax.random.fold_in(key, 6), dim), (parts,), jnp.float32, smallest / len(cuts), high / len(cuts))
        return jnp.repeat(jnp.exp(steps), dims[dim] // parts).reshape((-1,) + (1,) * (len(dims) - dim - 1))

    level = one(*cuts[0])
    for cut in cuts[1:]:
        level = level * one(*cut)
    return level


def centred(key, dims, spread, reach, pieces=(), kind=jnp.bfloat16):
    factor_of = levels(key, dims, pieces, -0.22, 0.18) if pieces else 1.0
    result = jax.random.normal(key, dims, jnp.float32) * spread * factor_of
    return jnp.minimum(jnp.maximum(result, -reach), reach).astype(kind)


def setup_inputs(seed: int = 0) -> dict:
    key_list = jax.random.split(jax.random.key(seed), 16)
    return {
        "hidden_in": draw_hidden_in(jax.random.fold_in(key_list[15], 71), 0),
        "attn_gain": jnp.clip(1.0 + 0.18 * jax.random.normal(key_list[1], (D,), jnp.float32), 0.099609375, 1.8984375).astype(jnp.bfloat16),
        "mlp_gain": jnp.clip(1.0 + 0.18 * jax.random.normal(key_list[2], (D,), jnp.float32), 0.099609375, 1.8984375).astype(jnp.bfloat16),
        "w_query": draw_w_query(jax.random.fold_in(key_list[15], 71), 0),
        "w_key": draw_w_key(jax.random.fold_in(key_list[15], 71), 0),
        "w_value": centred(key_list[5], (D, KVH * HD), D ** -0.5, 0.0625, ((0, 8), (1, 4))),
        "w_out": centred(key_list[6], (H * HD, D), (H * HD) ** -0.5, 0.0625, ((0, 4), (1, 8))),
        "w_gate": centred(key_list[7], (D, FF), D ** -0.5, 0.0625, ((1, 32),)),
        "w_up": centred(key_list[8], (D, FF), D ** -0.5, 0.0625, ((1, 32),)),
        "w_down": centred(key_list[9], (FF, D), FF ** -0.5, 0.03125, ((0, 32),)),
        "prompt_cache": draw_prompt_cache(jax.random.fold_in(key_list[15], 71), 0),
        "tail_cache": draw_tail_cache(jax.random.fold_in(key_list[15], 71), 0),
        "prompt_len": draw_prompt_len(jax.random.fold_in(key_list[15], 71), 0),
        "tail_len": draw_tail_len(jax.random.fold_in(key_list[15], 71), 0),
        "prompt_of": draw_prompt_of(jax.random.fold_in(key_list[15], 71), 0),
    }


EPS = 1e-05
THETA = 500000.0
NEG = -1e+30

def rope_table(position):
    half_width = HD // 2
    frequency = THETA ** (-(jnp.arange(half_width, dtype=jnp.float32) * 2.0 / HD))
    rotation = position.astype(jnp.float32)[:, None] * frequency[None, :]
    return (jnp.cos(rotation), jnp.sin(rotation))

def apply_rope(vectors, cosine, sine_table):
    half_width = vectors.shape[-1] // 2
    first_half = vectors[..., :half_width]
    second_half = vectors[..., half_width:]
    cos_rows = cosine[:, None, :]
    sin_rows = sine_table[:, None, :]
    return jnp.concatenate([first_half * cos_rows - second_half * sin_rows, second_half * cos_rows + first_half * sin_rows], axis=-1)

def masked_exp(scores, valid_mask, highest):
    return jnp.where(valid_mask, jnp.exp(jnp.where(valid_mask, scores, NEG) - highest[..., None]), 0.0)

def rounded(weights):
    return lax.optimization_barrier(weights.astype(jnp.bfloat16)).astype(jnp.float32)

def reference(hidden_in, attn_gain, mlp_gain, w_query, w_key, w_value, w_out, w_gate, w_up, w_down, prompt_cache, tail_cache, prompt_len, tail_len, prompt_of):
    wide_in = hidden_in.astype(jnp.float32)
    square_sum = lax.optimization_barrier(jnp.sum(wide_in * wide_in, axis=1))
    input_rms = jnp.sqrt(square_sum / D)
    inverse_rms = lax.rsqrt(square_sum / D + EPS)
    scaled_in = (wide_in * attn_gain.astype(jnp.float32)[None, :]).astype(jnp.bfloat16)
    query_sum = jnp.dot(scaled_in, w_query, preferred_element_type=jnp.float32) * inverse_rms[:, None]
    key_sum = jnp.dot(scaled_in, w_key, preferred_element_type=jnp.float32) * inverse_rms[:, None]
    value_new = (jnp.dot(scaled_in, w_value, preferred_element_type=jnp.float32) * inverse_rms[:, None]).astype(jnp.bfloat16).reshape(ROWS, KVH, HD)
    position = ((prompt_len[prompt_of] + tail_len)[:, None] + jnp.arange(2, dtype=jnp.int32)[None, :]).reshape(ROWS)
    cosine, sine_table = rope_table(position)
    query = apply_rope(query_sum.reshape(ROWS, H, HD), cosine, sine_table).astype(jnp.bfloat16)
    key_new = apply_rope(key_sum.reshape(ROWS, KVH, HD), cosine, sine_table).astype(jnp.bfloat16)
    new_entries = jnp.transpose(jnp.concatenate([key_new, value_new], axis=-1).reshape(REQ, 2, KVH, 2 * HD), (0, 2, 1, 3))
    order = jnp.argsort(prompt_of, stable=True).astype(jnp.int32)
    inverse_order = jnp.argsort(order).astype(jnp.int32)
    members = order.reshape(PROMPTS, CONT)
    query_grid = query.reshape(REQ, 2, KVH, QPK, HD)
    key_grid = key_new.reshape(REQ, 2, KVH, HD)
    value_grid = value_new.reshape(REQ, 2, KVH, HD)
    score_scale = HD ** (-0.5)
    step_mask = (jnp.arange(2)[None, :] <= jnp.arange(2)[:, None])[None, :, None, None, :]

    def one_prompt(inputs):
        prompt, chosen = inputs
        queries = query_grid[chosen].astype(jnp.float32)
        cache_block = lax.dynamic_index_in_dim(prompt_cache, prompt, 0, keepdims=False).astype(jnp.float32)
        prompt_scores = jnp.einsum('ntgqd,gjd->ntgqj', queries, cache_block[..., :HD]) * score_scale
        prompt_mask = (jnp.arange(PLEN, dtype=jnp.int32) < prompt_len[prompt])[None, None, None, None, :]
        tails = tail_cache[chosen].astype(jnp.float32)
        tail_scores = jnp.einsum('ntgqd,ngjd->ntgqj', queries, tails[..., :HD]) * score_scale
        tail_mask = (jnp.arange(TLEN, dtype=jnp.int32)[None, :] < tail_len[chosen][:, None])[:, None, None, None, :]
        self_keys = key_grid[chosen].astype(jnp.float32)
        self_values = value_grid[chosen].astype(jnp.float32)
        self_scores = jnp.einsum('ntgqd,nugd->ntgqu', queries, self_keys) * score_scale
        highest = jnp.maximum(jnp.maximum(lax.optimization_barrier(jnp.max(jnp.where(prompt_mask, prompt_scores, NEG), axis=-1)), lax.optimization_barrier(jnp.max(jnp.where(tail_mask, tail_scores, NEG), axis=-1))), lax.optimization_barrier(jnp.max(jnp.where(step_mask, self_scores, NEG), axis=-1)))
        prompt_weights = masked_exp(prompt_scores, prompt_mask, highest)
        tail_weights = masked_exp(tail_scores, tail_mask, highest)
        self_weights = masked_exp(self_scores, step_mask, highest)
        totals = lax.optimization_barrier(jnp.sum(prompt_weights, axis=-1)) + lax.optimization_barrier(jnp.sum(tail_weights, axis=-1)) + lax.optimization_barrier(jnp.sum(self_weights, axis=-1))
        accum = jnp.einsum('ntgqj,gjd->ntgqd', rounded(prompt_weights), cache_block[..., HD:])
        accum = accum + jnp.einsum('ntgqj,ngjd->ntgqd', rounded(tail_weights), tails[..., HD:])
        accum = accum + jnp.einsum('ntgqu,nugd->ntgqd', rounded(self_weights), self_values)
        return (accum / totals[..., None], highest)
    outputs, highs = lax.map(one_prompt, (jnp.arange(PROMPTS, dtype=jnp.int32), members))
    attention = outputs.reshape(REQ, 2, H, HD)[inverse_order].astype(jnp.bfloat16).reshape(ROWS, H * HD)
    max_logit = lax.optimization_barrier(jnp.max(highs.reshape(REQ, 2, H)[inverse_order], axis=1))
    head_whole = jnp.dot(attention, w_out, preferred_element_type=jnp.float32)
    residual = (wide_in + head_whole).astype(jnp.bfloat16)
    wide_mid = residual.astype(jnp.float32)
    inverse_mid = lax.rsqrt(lax.optimization_barrier(jnp.sum(wide_mid * wide_mid, axis=1)) / D + EPS)
    scaled_mid = (wide_mid * mlp_gain.astype(jnp.float32)[None, :]).astype(jnp.bfloat16)
    gate_value = jnp.dot(scaled_mid, w_gate, preferred_element_type=jnp.float32) * inverse_mid[:, None]
    up_value = jnp.dot(scaled_mid, w_up, preferred_element_type=jnp.float32) * inverse_mid[:, None]
    hidden = (jax.nn.silu(gate_value) * up_value).astype(jnp.bfloat16)
    layer_out = (wide_mid + jnp.dot(hidden, w_down, preferred_element_type=jnp.float32)).astype(jnp.bfloat16)
    return (layer_out, input_rms, max_logit, new_entries)
```

```python
import functools

import jax
import jax.numpy as jnp
from jax import lax
from jax.experimental import pallas as pl
from jax.experimental.pallas import tpu as pltpu
from jax.sharding import PartitionSpec as P

D = 8192
HD = 128
PROMPTS = 8
CONT = 16
QPK = 8
REQ = 128


EPS = 1e-05
THETA = 500000.0
NEG = -1e30
FLOOR = -1e29
MESH = pl.DeviceIdType.MESH


def rope_table(position, head_dim):
    half_width = head_dim // 2
    frequency = THETA ** (-(jnp.arange(half_width, dtype=jnp.float32) * 2.0 / head_dim))
    rotation = position.astype(jnp.float32)[:, None] * frequency[None, :]
    return (jnp.cos(rotation), jnp.sin(rotation))


def apply_rope(vectors, cosine, sine_table):
    half_width = vectors.shape[-1] // 2
    first_half = vectors[..., :half_width]
    second_half = vectors[..., half_width:]
    cos_rows = cosine[:, None, :]
    sin_rows = sine_table[:, None, :]
    return jnp.concatenate(
        [
            first_half * cos_rows - second_half * sin_rows,
            second_half * cos_rows + first_half * sin_rows,
        ],
        axis=-1,
    )


def merge_partials(earlier, later):
    top_early, total_early, accum_early = earlier
    top_late, total_late, accum_late = later
    highest = jnp.maximum(top_early, top_late)
    factor_early = jnp.exp(top_early - highest)
    factor_late = jnp.exp(top_late - highest)
    return (
        highest,
        total_early * factor_early + total_late * factor_late,
        accum_early * factor_early[..., None] + accum_late * factor_late[..., None],
    )


def softmax_terms(scores, valid_mask):
    masked = jnp.where(valid_mask, scores, NEG)
    highest = jnp.max(masked, axis=-1)
    weights = jnp.where(valid_mask, jnp.exp(masked - highest[..., None]), 0.0)
    return (highest, jnp.sum(weights, axis=-1), weights.astype(jnp.bfloat16))


def exchange_kernel(kinds, axis, stride, count, *refs):
    total = len(kinds)
    sources, targets = refs[:total], refs[total : 2 * total]
    send_sem, recv_sem, own_sem = refs[2 * total :]
    me = lax.axis_index(axis)
    place = lax.rem(lax.div(me, stride), count)
    base = me - place * stride
    barrier = pltpu.get_barrier_semaphore()
    for step in range(1, count):
        peer = base + lax.rem(place + step, count) * stride
        pl.semaphore_signal(barrier, inc=1, device_id={axis: peer}, device_id_type=MESH)
    pl.semaphore_wait(barrier, count - 1)
    copies = []
    for step in range(1, count):
        other = lax.rem(place + step, count)
        peer = base + other * stride
        for a in range(total):
            copy = pltpu.make_async_remote_copy(
                src_ref=sources[a].at[other] if kinds[a] == "scatter" else sources[a],
                dst_ref=targets[a].at[place],
                send_sem=send_sem.at[a, step],
                recv_sem=recv_sem.at[a, step],
                device_id={axis: peer},
                device_id_type=MESH,
            )
            copy.start()
            copies.append(copy)
    own = []
    for a in range(total):
        copy = pltpu.make_async_copy(
            sources[a].at[place] if kinds[a] == "scatter" else sources[a],
            targets[a].at[place],
            own_sem.at[a],
        )
        copy.start()
        own.append(copy)
    for copy in own + copies:
        copy.wait()


def exchange(arrays, kinds, axis, stride, count, identity):
    total = len(arrays)
    return pl.pallas_call(
        functools.partial(exchange_kernel, kinds, axis, stride, count),
        out_shape=[
            jax.ShapeDtypeStruct(a.shape if k == "scatter" else (count,) + a.shape, a.dtype)
            for a, k in zip(arrays, kinds)
        ],
        in_specs=[pl.BlockSpec(memory_space=pl.ANY)] * total,
        out_specs=[pl.BlockSpec(memory_space=pl.ANY)] * total,
        scratch_shapes=[
            pltpu.SemaphoreType.DMA((total, count)),
            pltpu.SemaphoreType.DMA((total, count)),
            pltpu.SemaphoreType.DMA((total,)),
        ],
        compiler_params=pltpu.CompilerParams(collective_id=identity, has_side_effects=True),
    )(*arrays)


def prompt_kernel(piece, length_ref, query_ref, cache_ref, accum_ref, stats_ref):
    length = length_ref[pl.program_id(0)]
    queries = query_ref[0, 0]
    rows = queries.shape[0]
    span = cache_ref.shape[2]
    top = jnp.full((rows, 1), FLOOR, jnp.float32)
    total = jnp.zeros((rows, 1), jnp.float32)
    accum = jnp.zeros((rows, HD), jnp.float32)
    for first in range(0, span, piece):
        keys = cache_ref[0, 0, first : first + piece, :HD]
        values = cache_ref[0, 0, first : first + piece, HD:]
        scores = lax.dot_general(
            queries, keys, (((1,), (1,)), ((), ())), preferred_element_type=jnp.float32
        ) * HD ** (-0.5)
        places = first + lax.broadcasted_iota(jnp.int32, (1, piece), 1)
        scores = jnp.where(places < length, scores, NEG)
        highest = jnp.maximum(top, jnp.max(scores, axis=1, keepdims=True))
        factor = jnp.exp(top - highest)
        weights = jnp.exp(scores - highest)
        total = total * factor + jnp.sum(weights, axis=1, keepdims=True)
        accum = accum * factor + jnp.dot(
            weights.astype(jnp.bfloat16), values, preferred_element_type=jnp.float32
        )
        top = highest
    accum_ref[0, 0] = accum.astype(jnp.bfloat16)
    lanes = lax.broadcasted_iota(jnp.int32, (rows, HD), 1)
    stats_ref[0, 0] = jnp.where(lanes < HD // 2, top, total)


def prompt_terms(queries, cache, lengths):
    prompts, heads, rows, _ = queries.shape
    span = cache.shape[2]
    piece = min(span, 1024)

    def place(p, g, lengths):
        return (p, g, 0, 0)

    return pl.pallas_call(
        functools.partial(prompt_kernel, piece),
        out_shape=[
            jax.ShapeDtypeStruct((prompts, heads, rows, HD), jnp.bfloat16),
            jax.ShapeDtypeStruct((prompts, heads, rows, HD), jnp.float32),
        ],
        grid_spec=pltpu.PrefetchScalarGridSpec(
            num_scalar_prefetch=1,
            grid=(prompts, heads),
            in_specs=[
                pl.BlockSpec((1, 1, rows, HD), place),
                pl.BlockSpec((1, 1, span, 2 * HD), place),
            ],
            out_specs=[
                pl.BlockSpec((1, 1, rows, HD), place),
                pl.BlockSpec((1, 1, rows, HD), place),
            ],
        ),
        compiler_params=pltpu.CompilerParams(vmem_limit_bytes=40 * 1024 * 1024),
        cost_estimate=pl.CostEstimate(
            flops=4 * prompts * heads * rows * span * HD,
            bytes_accessed=prompts * heads * span * HD * 4,
            transcendentals=prompts * heads * rows * span,
        ),
    )(lengths, queries, cache)


def shards(
    hidden_in,
    attn_gain,
    mlp_gain,
    w_query,
    w_key,
    w_value,
    w_out,
    w_gate,
    w_up,
    w_down,
    prompt_cache,
    tail_cache,
    prompt_len,
    tail_len,
    prompt_of,
):
    model_index = lax.axis_index("mp")
    seq_index = lax.axis_index("seq")
    model_count = lax.axis_size("mp")
    seq_count = lax.axis_size("seq")
    row_total = hidden_in.shape[0]
    kv_local = prompt_cache.shape[1]
    local_span = prompt_cache.shape[2]
    head_local = w_query.shape[1] // HD
    req_local = tail_cache.shape[0]
    tail_span = tail_cache.shape[2]
    row_share = row_total // (model_count * seq_count)
    score_scale = HD ** (-0.5)
    wide_in = hidden_in.astype(jnp.float32)
    scaled_in = (wide_in * attn_gain.astype(jnp.float32)[None, :]).astype(jnp.bfloat16)
    query_part = jnp.dot(scaled_in, w_query, preferred_element_type=jnp.float32)
    key_part = jnp.dot(scaled_in, w_key, preferred_element_type=jnp.float32)
    value_part = jnp.dot(scaled_in, w_value, preferred_element_type=jnp.float32)
    square_part = jnp.sum(wide_in * wide_in, axis=1)
    own_rows = row_total // model_count
    head_width = head_local * HD
    kv_width = kv_local * HD
    parts = jnp.concatenate([query_part, key_part, value_part], axis=1).astype(jnp.bfloat16)
    square_lanes = jnp.pad(square_part.reshape(row_total // HD, HD), ((0, 8 - row_total // HD), (0, 0)))
    part_all, square_all = exchange(
        [parts.reshape(model_count, own_rows, -1), square_lanes],
        ("scatter", "gather"), "mp", 1, model_count, 1,
    )
    sums = jnp.sum(part_all.astype(jnp.float32), axis=0)
    square_sum = jnp.sum(square_all, axis=0)[: row_total // HD].reshape(row_total)
    input_rms = jnp.sqrt(square_sum / D)
    inverse_rms = lax.rsqrt(square_sum / D + EPS)
    row_first = model_index * own_rows
    prompt_match = prompt_of[:, None] == jnp.arange(PROMPTS, dtype=jnp.int32)[None, :]
    prompt_start = jnp.sum(jnp.where(prompt_match, prompt_len[None, :], 0), axis=1)
    position = (
        (prompt_start + tail_len)[:, None] + jnp.arange(2, dtype=jnp.int32)[None, :]
    ).reshape(row_total)
    own_position = lax.dynamic_slice_in_dim(position, row_first, own_rows, 0)
    cosine, sine_table = rope_table(own_position, HD)
    sums = sums * lax.dynamic_slice_in_dim(inverse_rms, row_first, own_rows, 0)[:, None]
    query_rows = apply_rope(
        sums[:, :head_width].reshape(own_rows, head_local, HD), cosine, sine_table
    ).astype(jnp.bfloat16)
    own_keys = apply_rope(
        sums[:, head_width : head_width + kv_width].reshape(own_rows, kv_local, HD), cosine, sine_table
    ).astype(jnp.bfloat16)
    own_values = sums[:, head_width + kv_width :].astype(jnp.bfloat16).reshape(own_rows, kv_local, HD)
    entries = jnp.concatenate([own_keys, own_values], axis=-1).reshape(
        req_local, 2, kv_local, 2 * HD
    )
    new_entries = jnp.transpose(entries, (0, 2, 1, 3))
    (query_all,) = exchange(
        [query_rows.reshape(own_rows, head_width)], ("gather",), "mp", 1, model_count, 2
    )
    query = query_all.reshape(row_total, head_width)
    requests = jnp.arange(REQ, dtype=jnp.int32)
    ahead = (prompt_of[None, :] < prompt_of[:, None]) | (
        (prompt_of[None, :] == prompt_of[:, None]) & (requests[None, :] < requests[:, None])
    )
    rank = jnp.sum(ahead.astype(jnp.int32), axis=1)
    token_rank = (2 * rank[:, None] + jnp.arange(2, dtype=jnp.int32)[None, :]).reshape(row_total)
    moves = jnp.arange(row_total, dtype=jnp.int32)[:, None] == token_rank[None, :]
    moves_low = moves.astype(jnp.bfloat16)
    grouped = jnp.dot(moves_low, query, preferred_element_type=jnp.float32).astype(jnp.bfloat16)
    grouped = jnp.transpose(
        grouped.reshape(PROMPTS, CONT * 2, kv_local, QPK, HD), (0, 2, 1, 3, 4)
    ).reshape(PROMPTS, kv_local, CONT * 2 * QPK, HD)
    lengths = jnp.clip(prompt_len - model_index * local_span, 0, local_span)
    accum, stats = prompt_terms(grouped, prompt_cache, lengths)

    def token_rows(values):
        width = values.shape[-1]
        values = values.reshape(PROMPTS, kv_local, CONT * 2, QPK, width)
        return jnp.transpose(values, (0, 2, 1, 3, 4)).reshape(row_total, head_local * width)

    back = (((0,), (0,)), ((), ()))
    prompt_accum = lax.dot_general(
        moves_low, token_rows(accum), back, preferred_element_type=jnp.float32
    ).astype(jnp.bfloat16)
    stat_rows = jnp.concatenate(
        [token_rows(stats[..., :1]), token_rows(stats[..., HD // 2 : HD // 2 + 1])], axis=1
    )
    stat_rows = lax.dot_general(
        moves.astype(jnp.float32), stat_rows, back, precision=lax.Precision.HIGHEST,
        preferred_element_type=jnp.float32,
    )
    stat_rows = jnp.pad(stat_rows, ((0, 0), (0, HD - 2 * head_local)))
    accum_all, stat_all = exchange(
        [
            prompt_accum.reshape(model_count, own_rows, head_width),
            stat_rows.reshape(model_count, own_rows, HD),
        ],
        ("scatter", "scatter"), "mp", 1, model_count, 3,
    )
    own_query = query_rows.reshape(req_local, 2, kv_local, QPK, HD)
    own_tail = lax.dynamic_slice_in_dim(tail_len, model_index * req_local, req_local, 0)
    tail_scores = (
        jnp.einsum(
            "ntgqd,ngjd->ntgqj", own_query, tail_cache[..., :HD], preferred_element_type=jnp.float32
        )
        * score_scale
    )
    tail_mask = (jnp.arange(tail_span, dtype=jnp.int32)[None, :] < own_tail[:, None])[
        :, None, None, None, :
    ]
    tail_top, tail_total, tail_weights = softmax_terms(tail_scores, tail_mask)
    tail_accum = jnp.einsum(
        "ntgqj,ngjd->ntgqd", tail_weights, tail_cache[..., HD:], preferred_element_type=jnp.float32
    )
    self_keys = own_keys.reshape(req_local, 2, kv_local, HD)
    self_values = own_values.reshape(req_local, 2, kv_local, HD)
    self_scores = (
        jnp.einsum("ntgqd,nugd->ntgqu", own_query, self_keys, preferred_element_type=jnp.float32)
        * score_scale
    )
    step_mask = (
        jnp.arange(2, dtype=jnp.int32)[None, :] <= jnp.arange(2, dtype=jnp.int32)[:, None]
    )[None, :, None, None, :]
    self_top, self_total, self_weights = softmax_terms(self_scores, step_mask)
    self_accum = jnp.einsum(
        "ntgqu,nugd->ntgqd", self_weights, self_values, preferred_element_type=jnp.float32
    )
    own_top, own_total, own_accum = merge_partials(
        (tail_top, tail_total, tail_accum), (self_top, self_total, self_accum)
    )
    own_top = own_top.reshape(own_rows, head_local)
    own_total = own_total.reshape(own_rows, head_local)
    own_accum = own_accum.reshape(own_rows, head_local, HD)
    tops = stat_all[:, :, :head_local]
    totals = stat_all[:, :, head_local : 2 * head_local]
    merged_top = jnp.maximum(own_top, jnp.max(tops, axis=0))
    factors = jnp.exp(tops - merged_top[None])
    own_factor = jnp.exp(own_top - merged_top)
    merged_total = own_total * own_factor + jnp.sum(totals * factors, axis=0)
    merged_accum = own_accum * own_factor[..., None] + jnp.sum(
        accum_all.reshape(model_count, own_rows, head_local, HD).astype(jnp.float32)
        * factors[..., None],
        axis=0,
    )
    attention_rows = (
        (merged_accum / merged_total[..., None]).astype(jnp.bfloat16).reshape(own_rows, head_width)
    )
    own_max = jnp.max(merged_top.reshape(req_local, 2, head_local), axis=1)
    own_max = jnp.pad(own_max, ((0, 0), (0, HD - head_local)))
    attention_all, max_all = exchange(
        [attention_rows, own_max], ("gather", "gather"), "mp", 1, model_count, 4
    )
    attention = attention_all.reshape(row_total, head_width)
    max_logit = max_all.reshape(REQ, HD)[:, :head_local]
    head_part = jnp.dot(attention, w_out, preferred_element_type=jnp.float32)
    own_row = (model_index * seq_count + seq_index) * row_share
    seq_rows = row_total // seq_count
    cores, chips = 2, seq_count // 2
    (head_all,) = exchange(
        [head_part.reshape(seq_count, seq_rows, -1)], ("scatter",), "seq", 1, seq_count, 5
    )
    wide_rows = lax.dynamic_slice_in_dim(wide_in, seq_index * seq_rows, seq_rows, 0)
    residual = (wide_rows + jnp.sum(head_all, axis=0)).astype(jnp.bfloat16)
    (piece_model,) = exchange([residual], ("gather",), "mp", 1, model_count, 6)
    (piece_chip,) = exchange([piece_model], ("gather",), "seq", cores, chips, 7)
    (piece_core,) = exchange([piece_chip], ("gather",), "seq", 1, cores, 8)
    piece = jnp.transpose(piece_core, (1, 0, 3, 2, 4)).reshape(row_total, -1)
    wide_piece = piece.astype(jnp.float32)
    gain_piece = mlp_gain.astype(jnp.float32)
    scaled_piece = (wide_piece * gain_piece[None, :]).astype(jnp.bfloat16)
    gate_acc = jnp.dot(scaled_piece, w_gate, preferred_element_type=jnp.float32)
    up_acc = jnp.dot(scaled_piece, w_up, preferred_element_type=jnp.float32)
    square_acc = jnp.sum(wide_piece * wide_piece, axis=1)
    own_piece = lax.dynamic_slice_in_dim(piece, own_row, row_share, 0)
    own_block = own_piece
    gate_acc, up_acc, square_acc, own_block = (gate_acc, up_acc, square_acc, own_block)
    inverse_mid = lax.rsqrt(square_acc / D + EPS)
    gate_value = gate_acc * inverse_mid[:, None]
    up_value = up_acc * inverse_mid[:, None]
    hidden = (jax.nn.silu(gate_value) * up_value).astype(jnp.bfloat16)
    down = jnp.dot(hidden, w_down, preferred_element_type=jnp.float32).astype(jnp.bfloat16)
    down = jnp.transpose(
        down.reshape(model_count, chips, cores, row_share, D), (2, 1, 0, 3, 4)
    )
    (down_core,) = exchange(
        [down.reshape(cores, chips * model_count * row_share, D)], ("scatter",), "seq", 1, cores, 9
    )
    down = jnp.sum(down_core.astype(jnp.float32), axis=0).astype(jnp.bfloat16)
    (down_chip,) = exchange(
        [down.reshape(chips, model_count * row_share, D)], ("scatter",), "seq", cores, chips, 10
    )
    down = jnp.sum(down_chip.astype(jnp.float32), axis=0).astype(jnp.bfloat16)
    (down_model,) = exchange(
        [down.reshape(model_count, row_share * 8, D // 8)], ("scatter",), "mp", 1, model_count, 11
    )
    mlp_rows = jnp.sum(down_model.astype(jnp.float32), axis=0).reshape(row_share, D)
    layer_out = (own_block.astype(jnp.float32) + mlp_rows).astype(jnp.bfloat16)
    return (layer_out, input_rms, max_logit, new_entries)


def solution(mesh):
    in_specs = (
        P(None, "mp"),
        P("mp"),
        P(),
        P("mp", "seq"),
        P("mp", "seq"),
        P("mp", "seq"),
        P("seq", "mp"),
        P(None, ("mp", "seq")),
        P(None, ("mp", "seq")),
        P(("mp", "seq"), None),
        P(None, "seq", "mp", None),
        P("mp", "seq", None, None),
        P(),
        P(),
        P(),
    )
    out_specs = (P(("mp", "seq"), None), P(), P(None, "seq"), P("mp", "seq", None, None))
    return jax.shard_map(shards, mesh=mesh, in_specs=in_specs, out_specs=out_specs, check_vma=False)
```

```python
import functools

import jax
import jax.numpy as jnp
from jax import lax
from jax.experimental import pallas as pl
from jax.experimental.pallas import tpu as pltpu
from jax.sharding import PartitionSpec as P

D = 8192
HD = 128
PROMPTS = 8
CONT = 16
QPK = 8
REQ = 128


EPS = 1e-05
THETA = 500000.0
NEG = -1e30
FLOOR = -1e29
MESH = pl.DeviceIdType.MESH


def rope_table(position, head_dim):
    half_width = head_dim // 2
    frequency = THETA ** (-(jnp.arange(half_width, dtype=jnp.float32) * 2.0 / head_dim))
    rotation = position.astype(jnp.float32)[:, None] * frequency[None, :]
    return (jnp.cos(rotation), jnp.sin(rotation))


def apply_rope(vectors, cosine, sine_table):
    half_width = vectors.shape[-1] // 2
    first_half = vectors[..., :half_width]
    second_half = vectors[..., half_width:]
    cos_rows = cosine[:, None, :]
    sin_rows = sine_table[:, None, :]
    return jnp.concatenate(
        [
            first_half * cos_rows - second_half * sin_rows,
            second_half * cos_rows + first_half * sin_rows,
        ],
        axis=-1,
    )


def merge_partials(earlier, later):
    top_early, total_early, accum_early = earlier
    top_late, total_late, accum_late = later
    highest = jnp.maximum(top_early, top_late)
    factor_early = jnp.exp(top_early - highest)
    factor_late = jnp.exp(top_late - highest)
    return (
        highest,
        total_early * factor_early + total_late * factor_late,
        accum_early * factor_early[..., None] + accum_late * factor_late[..., None],
    )


def softmax_terms(scores, valid_mask):
    masked = jnp.where(valid_mask, scores, NEG)
    highest = jnp.max(masked, axis=-1)
    weights = jnp.where(valid_mask, jnp.exp(masked - highest[..., None]), 0.0)
    return (highest, jnp.sum(weights, axis=-1), weights.astype(jnp.bfloat16))


def exchange_kernel(kinds, axis, stride, count, cuts, *refs):
    total = len(kinds)
    sources, targets = refs[:total], refs[total : 2 * total]
    send_sem, recv_sem, own_sem = refs[2 * total :]
    me = lax.axis_index(axis)
    place = lax.rem(lax.div(me, stride), count)
    base = me - place * stride
    barrier = pltpu.get_barrier_semaphore()
    for step in range(1, count):
        peer = base + lax.rem(place + step, count) * stride
        pl.semaphore_signal(barrier, inc=1, device_id={axis: peer}, device_id_type=MESH)
    pl.semaphore_wait(barrier, count - 1)
    copies = []
    for step in range(1, count):
        other = lax.rem(place + step, count)
        peer = base + other * stride
        for a in range(total):
            span = targets[a].shape[1] // cuts
            for cut in range(cuts):
                part = pl.ds(cut * span, span)
                copy = pltpu.make_async_remote_copy(
                    src_ref=sources[a].at[other, part] if kinds[a] == "scatter" else sources[a].at[part],
                    dst_ref=targets[a].at[place, part],
                    send_sem=send_sem.at[a, step, cut],
                    recv_sem=recv_sem.at[a, step, cut],
                    device_id={axis: peer},
                    device_id_type=MESH,
                )
                copy.start()
                copies.append(copy)
    own = []
    for a in range(total):
        copy = pltpu.make_async_copy(
            sources[a].at[place] if kinds[a] == "scatter" else sources[a],
            targets[a].at[place],
            own_sem.at[a],
        )
        copy.start()
        own.append(copy)
    for copy in own + copies:
        copy.wait()


def exchange(arrays, kinds, axis, stride, count, identity, cuts=1):
    total = len(arrays)
    return pl.pallas_call(
        functools.partial(exchange_kernel, kinds, axis, stride, count, cuts),
        out_shape=[
            jax.ShapeDtypeStruct(a.shape if k == "scatter" else (count,) + a.shape, a.dtype)
            for a, k in zip(arrays, kinds)
        ],
        in_specs=[pl.BlockSpec(memory_space=pl.ANY)] * total,
        out_specs=[pl.BlockSpec(memory_space=pl.ANY)] * total,
        scratch_shapes=[
            pltpu.SemaphoreType.DMA((total, count, cuts)),
            pltpu.SemaphoreType.DMA((total, count, cuts)),
            pltpu.SemaphoreType.DMA((total,)),
        ],
        compiler_params=pltpu.CompilerParams(collective_id=identity, has_side_effects=True),
    )(*arrays)


def prompt_kernel(piece, length_ref, query_ref, cache_ref, accum_ref, stats_ref):
    length = length_ref[pl.program_id(0)]
    queries = query_ref[0, 0]
    rows = queries.shape[0]
    span = cache_ref.shape[2]
    top = jnp.full((rows, 1), FLOOR, jnp.float32)
    total = jnp.zeros((rows, 1), jnp.float32)
    accum = jnp.zeros((rows, HD), jnp.float32)
    for first in range(0, span, piece):
        keys = cache_ref[0, 0, first : first + piece, :HD]
        values = cache_ref[0, 0, first : first + piece, HD:]
        scores = lax.dot_general(
            queries, keys, (((1,), (1,)), ((), ())), preferred_element_type=jnp.float32
        ) * HD ** (-0.5)
        places = first + lax.broadcasted_iota(jnp.int32, (1, piece), 1)
        scores = jnp.where(places < length, scores, NEG)
        highest = jnp.maximum(top, jnp.max(scores, axis=1, keepdims=True))
        factor = jnp.exp(top - highest)
        weights = jnp.exp(scores - highest)
        total = total * factor + jnp.sum(weights, axis=1, keepdims=True)
        accum = accum * factor + jnp.dot(
            weights.astype(jnp.bfloat16), values, preferred_element_type=jnp.float32
        )
        top = highest
    accum_ref[0, 0] = accum.astype(jnp.bfloat16)
    lanes = lax.broadcasted_iota(jnp.int32, (rows, HD), 1)
    stats_ref[0, 0] = jnp.where(lanes < HD // 2, top, total)


def prompt_terms(queries, cache, lengths):
    prompts, heads, rows, _ = queries.shape
    span = cache.shape[2]
    piece = min(span, 1024)

    def place(p, g, lengths):
        return (p, g, 0, 0)

    return pl.pallas_call(
        functools.partial(prompt_kernel, piece),
        out_shape=[
            jax.ShapeDtypeStruct((prompts, heads, rows, HD), jnp.bfloat16),
            jax.ShapeDtypeStruct((prompts, heads, rows, HD), jnp.float32),
        ],
        grid_spec=pltpu.PrefetchScalarGridSpec(
            num_scalar_prefetch=1,
            grid=(prompts, heads),
            in_specs=[
                pl.BlockSpec((1, 1, rows, HD), place),
                pl.BlockSpec((1, 1, span, 2 * HD), place),
            ],
            out_specs=[
                pl.BlockSpec((1, 1, rows, HD), place),
                pl.BlockSpec((1, 1, rows, HD), place),
            ],
        ),
        compiler_params=pltpu.CompilerParams(vmem_limit_bytes=40 * 1024 * 1024),
        cost_estimate=pl.CostEstimate(
            flops=4 * prompts * heads * rows * span * HD,
            bytes_accessed=prompts * heads * span * HD * 4,
            transcendentals=prompts * heads * rows * span,
        ),
    )(lengths, queries, cache)


def shards(
    hidden_in,
    attn_gain,
    mlp_gain,
    w_query,
    w_key,
    w_value,
    w_out,
    w_gate,
    w_up,
    w_down,
    prompt_cache,
    tail_cache,
    prompt_len,
    tail_len,
    prompt_of,
):
    model_index = lax.axis_index("mp")
    seq_index = lax.axis_index("seq")
    model_count = lax.axis_size("mp")
    seq_count = lax.axis_size("seq")
    row_total = hidden_in.shape[0]
    kv_local = prompt_cache.shape[1]
    local_span = prompt_cache.shape[2]
    head_local = w_query.shape[1] // HD
    req_local = tail_cache.shape[0]
    tail_span = tail_cache.shape[2]
    row_share = row_total // (model_count * seq_count)
    score_scale = HD ** (-0.5)
    wide_in = hidden_in.astype(jnp.float32)
    scaled_in = (wide_in * attn_gain.astype(jnp.float32)[None, :]).astype(jnp.bfloat16)
    query_part = jnp.dot(scaled_in, w_query, preferred_element_type=jnp.float32)
    key_part = jnp.dot(scaled_in, w_key, preferred_element_type=jnp.float32)
    value_part = jnp.dot(scaled_in, w_value, preferred_element_type=jnp.float32)
    square_part = jnp.sum(wide_in * wide_in, axis=1)
    own_rows = row_total // model_count
    head_width = head_local * HD
    kv_width = kv_local * HD
    entry_part = jnp.concatenate([key_part, value_part], axis=1)
    square_lanes = jnp.pad(square_part.reshape(row_total // HD, HD), ((0, 8 - row_total // HD), (0, 0)))
    part_all, entry_all, square_all = exchange(
        [
            query_part.astype(jnp.bfloat16).reshape(model_count, own_rows, -1),
            entry_part.reshape(model_count, own_rows, -1),
            square_lanes,
        ],
        ("scatter", "scatter", "gather"), "mp", 1, model_count, 1,
    )
    query_sum = jnp.sum(part_all.astype(jnp.float32), axis=0)
    entry_sum = jnp.sum(entry_all, axis=0)
    square_sum = jnp.sum(square_all, axis=0)[: row_total // HD].reshape(row_total)
    input_rms = jnp.sqrt(square_sum / D)
    inverse_rms = lax.rsqrt(square_sum / D + EPS)
    row_first = model_index * own_rows
    prompt_match = prompt_of[:, None] == jnp.arange(PROMPTS, dtype=jnp.int32)[None, :]
    prompt_start = jnp.sum(jnp.where(prompt_match, prompt_len[None, :], 0), axis=1)
    position = (
        (prompt_start + tail_len)[:, None] + jnp.arange(2, dtype=jnp.int32)[None, :]
    ).reshape(row_total)
    own_position = lax.dynamic_slice_in_dim(position, row_first, own_rows, 0)
    cosine, sine_table = rope_table(own_position, HD)
    own_inverse = lax.dynamic_slice_in_dim(inverse_rms, row_first, own_rows, 0)[:, None]
    query_sum = query_sum * own_inverse
    entry_sum = entry_sum * own_inverse
    query_rows = apply_rope(
        query_sum.reshape(own_rows, head_local, HD), cosine, sine_table
    ).astype(jnp.bfloat16)
    own_keys = apply_rope(
        entry_sum[:, :kv_width].reshape(own_rows, kv_local, HD), cosine, sine_table
    ).astype(jnp.bfloat16)
    own_values = entry_sum[:, kv_width:].astype(jnp.bfloat16).reshape(own_rows, kv_local, HD)
    entries = jnp.concatenate([own_keys, own_values], axis=-1).reshape(
        req_local, 2, kv_local, 2 * HD
    )
    new_entries = jnp.transpose(entries, (0, 2, 1, 3))
    (query_all,) = exchange(
        [query_rows.reshape(own_rows, head_width)], ("gather",), "mp", 1, model_count, 2
    )
    query = query_all.reshape(row_total, head_width)
    requests = jnp.arange(REQ, dtype=jnp.int32)
    ahead = (prompt_of[None, :] < prompt_of[:, None]) | (
        (prompt_of[None, :] == prompt_of[:, None]) & (requests[None, :] < requests[:, None])
    )
    rank = jnp.sum(ahead.astype(jnp.int32), axis=1)
    token_rank = (2 * rank[:, None] + jnp.arange(2, dtype=jnp.int32)[None, :]).reshape(row_total)
    moves = jnp.arange(row_total, dtype=jnp.int32)[:, None] == token_rank[None, :]
    moves_low = moves.astype(jnp.bfloat16)
    grouped = jnp.dot(moves_low, query, preferred_element_type=jnp.float32).astype(jnp.bfloat16)
    grouped = jnp.transpose(
        grouped.reshape(PROMPTS, CONT * 2, kv_local, QPK, HD), (0, 2, 1, 3, 4)
    ).reshape(PROMPTS, kv_local, CONT * 2 * QPK, HD)
    lengths = jnp.clip(prompt_len - model_index * local_span, 0, local_span)
    accum, stats = prompt_terms(grouped, prompt_cache, lengths)

    def token_rows(values):
        width = values.shape[-1]
        values = values.reshape(PROMPTS, kv_local, CONT * 2, QPK, width)
        return jnp.transpose(values, (0, 2, 1, 3, 4)).reshape(row_total, head_local * width)

    back = (((0,), (0,)), ((), ()))
    prompt_accum = lax.dot_general(
        moves_low, token_rows(accum), back, preferred_element_type=jnp.float32
    ).astype(jnp.bfloat16)
    stat_rows = jnp.concatenate(
        [token_rows(stats[..., :1]), token_rows(stats[..., HD // 2 : HD // 2 + 1])], axis=1
    )
    stat_rows = lax.dot_general(
        moves.astype(jnp.float32), stat_rows, back, precision=lax.Precision.HIGHEST,
        preferred_element_type=jnp.float32,
    )
    stat_rows = jnp.pad(stat_rows, ((0, 0), (0, HD - 2 * head_local)))
    accum_all, stat_all = exchange(
        [
            prompt_accum.reshape(model_count, own_rows, head_width),
            stat_rows.reshape(model_count, own_rows, HD),
        ],
        ("scatter", "scatter"), "mp", 1, model_count, 3,
    )
    own_query = query_rows.reshape(req_local, 2, kv_local, QPK, HD)
    own_tail = lax.dynamic_slice_in_dim(tail_len, model_index * req_local, req_local, 0)
    tail_scores = (
        jnp.einsum(
            "ntgqd,ngjd->ntgqj", own_query, tail_cache[..., :HD], preferred_element_type=jnp.float32
        )
        * score_scale
    )
    tail_mask = (jnp.arange(tail_span, dtype=jnp.int32)[None, :] < own_tail[:, None])[
        :, None, None, None, :
    ]
    tail_top, tail_total, tail_weights = softmax_terms(tail_scores, tail_mask)
    tail_accum = jnp.einsum(
        "ntgqj,ngjd->ntgqd", tail_weights, tail_cache[..., HD:], preferred_element_type=jnp.float32
    )
    self_keys = own_keys.reshape(req_local, 2, kv_local, HD)
    self_values = own_values.reshape(req_local, 2, kv_local, HD)
    self_scores = (
        jnp.einsum("ntgqd,nugd->ntgqu", own_query, self_keys, preferred_element_type=jnp.float32)
        * score_scale
    )
    step_mask = (
        jnp.arange(2, dtype=jnp.int32)[None, :] <= jnp.arange(2, dtype=jnp.int32)[:, None]
    )[None, :, None, None, :]
    self_top, self_total, self_weights = softmax_terms(self_scores, step_mask)
    self_accum = jnp.einsum(
        "ntgqu,nugd->ntgqd", self_weights, self_values, preferred_element_type=jnp.float32
    )
    own_top, own_total, own_accum = merge_partials(
        (tail_top, tail_total, tail_accum), (self_top, self_total, self_accum)
    )
    own_top = own_top.reshape(own_rows, head_local)
    own_total = own_total.reshape(own_rows, head_local)
    own_accum = own_accum.reshape(own_rows, head_local, HD)
    tops = stat_all[:, :, :head_local]
    totals = stat_all[:, :, head_local : 2 * head_local]
    merged_top = jnp.maximum(own_top, jnp.max(tops, axis=0))
    factors = jnp.exp(tops - merged_top[None])
    own_factor = jnp.exp(own_top - merged_top)
    merged_total = own_total * own_factor + jnp.sum(totals * factors, axis=0)
    merged_accum = own_accum * own_factor[..., None] + jnp.sum(
        accum_all.reshape(model_count, own_rows, head_local, HD).astype(jnp.float32)
        * factors[..., None],
        axis=0,
    )
    attention_rows = (
        (merged_accum / merged_total[..., None]).astype(jnp.bfloat16).reshape(own_rows, head_width)
    )
    own_max = jnp.max(merged_top.reshape(req_local, 2, head_local), axis=1)
    own_max = jnp.pad(own_max, ((0, 0), (0, HD - head_local)))
    attention_all, max_all = exchange(
        [attention_rows, own_max], ("gather", "gather"), "mp", 1, model_count, 4
    )
    attention = attention_all.reshape(row_total, head_width)
    max_logit = max_all.reshape(REQ, HD)[:, :head_local]
    head_part = jnp.dot(attention, w_out, preferred_element_type=jnp.float32)
    own_row = (model_index * seq_count + seq_index) * row_share
    seq_rows = row_total // seq_count
    (head_all,) = exchange(
        [head_part.reshape(seq_count, seq_rows, -1)], ("scatter",), "seq", 1, seq_count, 5
    )
    wide_rows = lax.dynamic_slice_in_dim(wide_in, seq_index * seq_rows, seq_rows, 0)
    residual = (wide_rows + jnp.sum(head_all, axis=0)).astype(jnp.bfloat16)
    (piece_model,) = exchange([residual], ("gather",), "mp", 1, model_count, 6)
    (piece_all,) = exchange([piece_model], ("gather",), "seq", 1, seq_count, 7)
    piece = jnp.transpose(piece_all, (0, 2, 1, 3)).reshape(row_total, -1)
    wide_piece = piece.astype(jnp.float32)
    gain_piece = mlp_gain.astype(jnp.float32)
    scaled_piece = (wide_piece * gain_piece[None, :]).astype(jnp.bfloat16)
    gate_acc = jnp.dot(scaled_piece, w_gate, preferred_element_type=jnp.float32)
    up_acc = jnp.dot(scaled_piece, w_up, preferred_element_type=jnp.float32)
    square_acc = jnp.sum(wide_piece * wide_piece, axis=1)
    own_piece = lax.dynamic_slice_in_dim(piece, own_row, row_share, 0)
    own_block = own_piece
    gate_acc, up_acc, square_acc, own_block = (gate_acc, up_acc, square_acc, own_block)
    inverse_mid = lax.rsqrt(square_acc / D + EPS)
    gate_value = gate_acc * inverse_mid[:, None]
    up_value = up_acc * inverse_mid[:, None]
    hidden = (jax.nn.silu(gate_value) * up_value).astype(jnp.bfloat16)
    down = jnp.dot(hidden, w_down, preferred_element_type=jnp.float32).astype(jnp.bfloat16)
    down = jnp.transpose(down.reshape(model_count, seq_count, row_share, D), (1, 0, 2, 3))
    (down_seq,) = exchange(
        [down.reshape(seq_count, model_count * row_share, D)], ("scatter",), "seq", 1, seq_count, 9
    )
    down = jnp.sum(down_seq.astype(jnp.float32), axis=0).astype(jnp.bfloat16)
    (down_model,) = exchange(
        [down.reshape(model_count, row_share * 8, D // 8)], ("scatter",), "mp", 1, model_count, 11
    )
    mlp_rows = jnp.sum(down_model.astype(jnp.float32), axis=0).reshape(row_share, D)
    layer_out = (own_block.astype(jnp.float32) + mlp_rows).astype(jnp.bfloat16)
    return (layer_out, input_rms, max_logit, new_entries)


def solution(mesh):
    in_specs = (
        P(None, "mp"),
        P("mp"),
        P(),
        P("mp", "seq"),
        P("mp", "seq"),
        P("mp", "seq"),
        P("seq", "mp"),
        P(None, ("mp", "seq")),
        P(None, ("mp", "seq")),
        P(("mp", "seq"), None),
        P(None, "seq", "mp", None),
        P("mp", "seq", None, None),
        P(),
        P(),
        P(),
    )
    out_specs = (P(("mp", "seq"), None), P(), P(None, "seq"), P("mp", "seq", None, None))
    return jax.shard_map(shards, mesh=mesh, in_specs=in_specs, out_specs=out_specs, check_vma=False)
```
